32 devices in a mesh: row: 4 (over z), col: 8 (over y, x, core).
Axes of the slice: x: 2, y: 2, z: 4, core: 2. Of those that a mesh axis runs over, the one named last changes fastest.
Arguments:
- tokens: bfloat16 [1024, 2560], P('row', 'col'), may hold values from -6 to 6
- w_down: bfloat16 [2560, 1056], P('col'), may hold values from -0.125 to 0.125
- q_gain: float32 [768], replicated, may hold values from 0.1 to 1.9
- kv_gain: float32 [256], replicated, may hold values from 0.1 to 1.9
- w_q_up: bfloat16 [768, 768], P(None, 'col'), may hold values from -8.8767604 to 8.8767604
- w_kv_up: bfloat16 [256, 1024], replicated, may hold values from -0.375 to 0.375
- w_out: bfloat16 [512, 2560], P('col'), may hold values from -0.75 to 0.75
- latent_cache: bfloat16 [4, 2048, 288], P('row', 'col'), may hold values from -6 to 6
- cache_len: int32 [4], replicated, may hold values from 1 to 2048, as said below
- new_len: int32 [4], replicated, may hold values from 1 to 256, as said below
- page_table: int32 [4, 32], replicated, may hold values from 0 to 31, each once within a row
- home_slot: int32 [4], replicated, may hold values from 0 to 3, each once
Outputs:
- output: bfloat16 [1024, 2560], P('row', 'col')
The draws below stay inside these ranges and needn't reach their ends.
Inputs may be any that keep to these rules, and one draw needn't show every extreme that they name: `cache_len`: some slot has exactly 2048 cached tokens; about half the slots hold at most 256, the others at least 1792. `new_len`: some request has exactly 256 real new tokens.
All inputs are finite; a program needn't handle non-finite values.
Results may differ from the reference program's by a relative error of at most 0.023.
Values may be sent and summed in bfloat16 or wider, within the bound.
No kernel may reach another device: no remote copies, remote signals or barrier semaphores. Data moves between devices by JAX's collectives and lax.ppermute only.
A program may use at most 64 MiB of HBM per device.

```python
import math
import jax
import jax.numpy as jnp
from jax import lax

D = 2560
QR = 768
KR = 256
NOPE = 64
ROPE = 32
VDIM = 64
GROUP = 256
PAGE = 64
HEADS = 8
R = 4
NPAGE = 32
MAXC = 2048
TOKENS = 1024


def draw_w_q_up(key, part):
    key_base = jax.random.fold_in(key, 11)
    base_draw = jnp.clip(jax.random.normal(key_base, (QR, HEADS * (NOPE + ROPE)), jnp.float32), -6.0, 6.0) * QR ** (-0.5)
    return base_draw.astype(jnp.bfloat16)


def draw_cache_len(key, part):
    key_short = jax.random.fold_in(key, 21)
    key_long = jax.random.fold_in(key, 22)
    key_pick = jax.random.fold_in(key, 23)
    key_fill = jax.random.fold_in(key, 24)
    shorter = jax.random.randint(key_short, (R,), 1, MAXC // 8 + 1)
    longer = MAXC - jax.random.randint(key_long, (R,), 0, MAXC // 8 + 1)
    picked = jax.random.randint(key_pick, (R,), 0, 2)
    lengths = jnp.where(picked == 1, longer, shorter)
    fullest = jax.random.randint(key_fill, (), 0, R)
    return jnp.where(jnp.arange(R) == fullest, MAXC, lengths).astype(jnp.int32)


def draw_new_len(key, part):
    key_length = jax.random.fold_in(key, 31)
    key_fill = jax.random.fold_in(key, 32)
    lengths = jax.random.randint(key_length, (R,), GROUP // 4 + 1, GROUP + 1)
    fullest = jax.random.randint(key_fill, (), 0, R)
    return jnp.where(jnp.arange(R) == fullest, GROUP, lengths).astype(jnp.int32)


def levels(rng, dims, split, least, largest):
    def one(axis_at, blocks):
        heights = jax.random.uniform(jax.random.fold_in(jax.random.fold_in(rng, 6), axis_at), (blocks,), jnp.float32, least / len(split), largest / len(split))
        return jnp.repeat(jnp.exp(heights), dims[axis_at] // blocks).reshape((-1,) + (1,) * (len(dims) - axis_at - 1))

    loudness = one(*split[0])
    for cut in split[1:]:
        loudness = loudness * one(*cut)
    return loudness


def normal_values(own_key, dims, deviation, reach, shards=(), held_as=jnp.bfloat16):
    level = levels(own_key, dims, shards, -0.22, 0.18) if shards else 1.0
    entries = jax.random.normal(own_key, dims, jnp.float32) * deviation * level
    return jnp.minimum(jnp.maximum(entries, -reach), reach).astype(held_as)


def setup_inputs(seed: int = 0) -> dict:
    seeds = jax.random.split(jax.random.key(seed), 13)
    return {
        "tokens": normal_values(seeds[0], (TOKENS, D), 1.0, 6.0, ((0, 4), (1, 8))),
        "w_down": normal_values(seeds[1], (D, QR + KR + ROPE), D ** -0.5, 0.125, ((0, 8),)),
        "q_gain": jnp.clip(1.0 + 0.18 * jax.random.normal(seeds[2], (QR,), jnp.float32), 0.1, 1.9),
        "kv_gain": jnp.clip(1.0 + 0.18 * jax.random.normal(seeds[3], (KR,), jnp.float32), 0.1, 1.9),
        "w_q_up": draw_w_q_up(jax.random.fold_in(seeds[12], 71), 0),
        "w_kv_up": normal_values(seeds[5], (KR, HEADS * (NOPE + VDIM)), KR ** -0.5, 0.375),
        "w_out": normal_values(seeds[6], (HEADS * VDIM, D), VDIM ** -0.5, 0.75, ((0, 8),)),
        "latent_cache": normal_values(seeds[7], (R, MAXC, KR + ROPE), 1.0, 6.0, ((0, 4), (1, 8))),
        "cache_len": draw_cache_len(jax.random.fold_in(seeds[12], 71), 0),
        "new_len": draw_new_len(jax.random.fold_in(seeds[12], 71), 0),
        "page_table": jax.vmap(lambda own: jax.random.permutation(own, NPAGE))(jax.random.split(seeds[10], R)).reshape((R, NPAGE)).astype(jnp.int32),
        "home_slot": jax.random.permutation(seeds[11], R).astype(jnp.int32),
    }


epsilon = 1e-05

def rms_scale(values, gain):
    return values * lax.rsqrt(lax.optimization_barrier(jnp.mean(values * values, axis=-1, keepdims=True)) + epsilon) * gain

def angle_tables(positions, width):
    half_dim = width // 2
    frequency = 10000.0 ** (-2.0 * jnp.arange(half_dim, dtype=jnp.float32) / width)
    angles = positions.astype(jnp.float32)[:, None] * frequency[None, :]
    return (jnp.cos(angles), jnp.sin(angles))

def rotary(values, cosine, sine_table):
    half_dim = values.shape[-1] // 2
    first_half = values[..., :half_dim]
    second_half = values[..., half_dim:]
    return jnp.concatenate([first_half * cosine - second_half * sine_table, second_half * cosine + first_half * sine_table], -1)

def reference(tokens, w_down, q_gain, kv_gain, w_q_up, w_kv_up, w_out, latent_cache, cache_len, new_len, page_table, home_slot):
    combined = jnp.dot(tokens, w_down, preferred_element_type=jnp.float32)
    block_of = jnp.arange(TOKENS, dtype=jnp.int32) // GROUP
    within = jnp.arange(TOKENS, dtype=jnp.int32) % GROUP
    position = cache_len[home_slot[block_of]] + within
    cosine, sine_table = angle_tables(position, ROPE)
    query_latent = rms_scale(combined[:, :QR], q_gain).astype(jnp.bfloat16)
    new_latent = rms_scale(combined[:, QR:QR + KR], kv_gain).astype(jnp.bfloat16)
    new_rope = rotary(combined[:, QR + KR:], cosine, sine_table).astype(jnp.bfloat16)
    projected = jnp.dot(query_latent, w_q_up, preferred_element_type=jnp.float32).reshape(TOKENS, HEADS, NOPE + ROPE)
    queries = jnp.concatenate([projected[..., :NOPE], rotary(projected[..., NOPE:], cosine[:, None, :], sine_table[:, None, :])], -1).astype(jnp.bfloat16)
    new_rows = jnp.concatenate([new_latent, new_rope], 1)
    score_scale = 1.0 / math.sqrt(NOPE + ROPE)
    key_count = MAXC + GROUP
    outputs = []
    for block_id in range(R):
        slot_index = home_slot[block_id]
        latents = jnp.concatenate([latent_cache[slot_index], new_rows[block_id * GROUP:(block_id + 1) * GROUP]], 0)
        lifted = jnp.dot(latents[:, :KR], w_kv_up, preferred_element_type=jnp.float32).astype(jnp.bfloat16).reshape(key_count, HEADS, NOPE + VDIM)
        key_rows = jnp.concatenate([lifted[..., :NOPE], jnp.broadcast_to(latents[:, None, KR:], (key_count, HEADS, ROPE))], -1)
        values = lifted[..., NOPE:]
        page_row = page_table[slot_index]
        page_ids = jnp.arange(NPAGE, dtype=jnp.int32)
        logical_page = lax.optimization_barrier(jnp.sum(page_ids[:, None] * (page_row[:, None] == page_ids[None, :]).astype(jnp.int32), 0))
        logical = (logical_page[:, None] * PAGE + jnp.arange(PAGE, dtype=jnp.int32)[None, :]).reshape(MAXC)
        cached_seen = logical < cache_len[slot_index]
        query_index = jnp.arange(GROUP, dtype=jnp.int32)[:, None]
        key_index = jnp.arange(GROUP, dtype=jnp.int32)[None, :]
        new_seen = (key_index <= query_index) & (key_index < new_len[block_id])
        visible = jnp.concatenate([jnp.broadcast_to(cached_seen[None, :], (GROUP, MAXC)), new_seen], 1)
        block_query = queries[block_id * GROUP:(block_id + 1) * GROUP].astype(jnp.float32)
        scores = jnp.einsum('qhd,khd->hqk', block_query, key_rows.astype(jnp.float32)) * score_scale
        scores = jnp.where(visible[None], scores, -jnp.inf)
        row_peak = lax.optimization_barrier(jnp.max(scores, -1, keepdims=True))
        exponent = jnp.exp(scores - row_peak)
        row_total = lax.optimization_barrier(jnp.sum(exponent, -1))
        weights = exponent.astype(jnp.bfloat16)
        summed = jnp.einsum('hqk,khd->qhd', weights.astype(jnp.float32), values.astype(jnp.float32))
        attended = (summed / row_total.T[:, :, None]).astype(jnp.bfloat16)
        live_rows = jnp.arange(GROUP, dtype=jnp.int32) < new_len[block_id]
        attended = jnp.where(live_rows[:, None, None], attended, jnp.zeros_like(attended))
        outputs.append(attended.reshape(GROUP, HEADS * VDIM))
    attended_all = jnp.concatenate(outputs, 0)
    return jnp.dot(attended_all, w_out, preferred_element_type=jnp.float32).astype(jnp.bfloat16)
```

```python
import functools
import math

import jax
import jax.numpy as jnp
from jax import lax
from jax.experimental import pallas as pl
from jax.experimental.pallas import tpu as pltpu
from jax.sharding import PartitionSpec as P

NOPE = 64
ROPE = 32
VDIM = 64
HEAD = NOPE + VDIM
SPAN = 4
epsilon = 1e-05
MASKED = -1e30
FLOOR = -1e29

bf16 = jnp.bfloat16
f32 = jnp.float32
VMEM = pl.BlockSpec(memory_space=pltpu.VMEM)
SMEM = pl.BlockSpec(memory_space=pltpu.SMEM)
PARAMS = pltpu.CompilerParams(vmem_limit_bytes=32 * 1024 * 1024)


def cost(flops, moved, special=0):
    return pl.CostEstimate(flops=flops, bytes_accessed=moved, transcendentals=special)


def angle_tables(positions, width):
    half_dim = width // 2
    frequency = 10000.0 ** (-2.0 * jnp.arange(half_dim, dtype=f32) / width)
    angles = positions.astype(f32)[:, None] * frequency[None, :]
    return (jnp.cos(angles), jnp.sin(angles))


def rotate(values, cosine, sine):
    half = ROPE // 2
    first, second = values[:, :half], values[:, half:]
    return jnp.concatenate(
        [first * cosine - second * sine, second * cosine + first * sine], axis=1
    )


def down_kernel(count, own, tokens_ref, w_ref, even_ref, odd_ref, sums):
    column = lax.axis_index("col")
    sums[...] = jnp.dot(tokens_ref[...], w_ref[...], preferred_element_type=f32)
    for j in range(count):
        start = pl.multiple_of((column ^ j) * own, own)
        target = odd_ref if j % 2 else even_ref
        target[j // 2] = sums[pl.ds(start, own), :].astype(bf16)


def norm_kernel(own, q_width, kv_width, cos_ref, sin_ref, q_gain_ref, kv_gain_ref, *refs):
    out_ref = refs[-1]
    column = lax.axis_index("col")
    total = refs[0][...].astype(f32)
    for ref in refs[1:-1]:
        total += ref[...].astype(f32)

    def scaled(values, gain):
        mean = jnp.mean(values * values, axis=-1, keepdims=True)
        return values * lax.rsqrt(mean + epsilon) * gain

    rows = pl.ds(pl.multiple_of(column * own, own), own)
    out_ref[:, :q_width] = scaled(total[:, :q_width], q_gain_ref[...]).astype(bf16)
    out_ref[:, q_width : q_width + kv_width] = scaled(
        total[:, q_width : q_width + kv_width], kv_gain_ref[...]
    ).astype(bf16)
    out_ref[:, q_width + kv_width :] = rotate(
        total[:, q_width + kv_width :], cos_ref[rows, :], sin_ref[rows, :]
    ).astype(bf16)


def split3(value):
    high = value.astype(bf16)
    rest = value - high.astype(f32)
    middle = rest.astype(bf16)
    low = (rest - middle.astype(f32)).astype(bf16)
    return [high, middle, low]


def attend_kernel(
    span, count, own, q_width, kv_width, merged,
    home_ref, cached_ref, live_ref, page_ref, cos_ref, sin_ref, w_kv_ref, *refs,
):
    heads = count // span
    weights, refs = refs[:heads], refs[heads:]
    blocks, refs = refs[:count], refs[count:]
    pieces, refs = refs[:span], refs[span:]
    outs, (query_rows, fresh, keys, limits) = refs[:-4], refs[-4:]
    column = lax.axis_index("col")
    slot = home_ref[lax.axis_index("row")]
    live = live_ref[lax.axis_index("row")]
    cached = cached_ref[slot]
    group = count * own
    piece = pieces[0].shape[0]
    page_count = page_ref.shape[1]
    page = piece * count // page_count
    held = piece * span
    for j in range(count):
        start = pl.multiple_of((column ^ j) * own, own)
        query_rows[pl.ds(start, own), :] = blocks[j][:, :q_width].astype(f32)
        if j < span:
            fresh[j * own : (j + 1) * own, :] = blocks[j][:, q_width:].astype(f32)
    for j in range(span):
        keys[j * piece : (j + 1) * piece, :] = pieces[j][...]
        offset = lax.broadcasted_iota(jnp.int32, (1, piece), 1)
        position = (column ^ j) * piece + offset
        page_id = position // page
        logical = jnp.zeros((1, piece), jnp.int32)
        for l in range(page_count):
            logical = jnp.where(page_id == page_ref[slot, l], l, logical)
        seen = logical * page + offset % page < cached
        limits[:, j * piece : (j + 1) * piece] = jnp.where(seen, 0.0, MASKED)
    keys[held:, :] = fresh[...].astype(bf16)
    query_id = lax.broadcasted_iota(jnp.int32, (group, span * own), 0)
    fresh_lane = lax.broadcasted_iota(jnp.int32, (1, span * own), 1)
    fresh_id = (column ^ (fresh_lane // own)) * own + fresh_lane % own
    fresh_bias = jnp.where((fresh_id <= query_id) & (fresh_id < live), 0.0, MASKED)
    latent = query_rows[...].astype(bf16)
    scale = 1.0 / math.sqrt(NOPE + ROPE)
    for k in range(heads):
        head = column ^ (k * span)
        lift = w_kv_ref[:, pl.ds(pl.multiple_of(head * HEAD, HEAD), HEAD)]
        projected = jnp.dot(latent, weights[k][...], preferred_element_type=f32)
        turned = rotate(projected[:, NOPE:], cos_ref[...], sin_ref[...]).astype(bf16)
        plain = lax.dot_general(
            projected[:, :NOPE].astype(bf16), lift[:, :NOPE],
            (((1,), (1,)), ((), ())), preferred_element_type=f32,
        ).astype(bf16)
        query = jnp.concatenate([plain, turned], axis=1)
        scores = lax.dot_general(
            query, keys[...], (((1,), (1,)), ((), ())), preferred_element_type=f32
        )
        old = scores[:, :held] + limits[...]
        new = scores[:, held:] + fresh_bias
        peak = jnp.maximum(jnp.max(old, 1, keepdims=True), jnp.max(new, 1, keepdims=True))
        peak = jnp.maximum(peak, FLOOR)
        old = jnp.exp((old - peak) * scale)
        new = jnp.exp((new - peak) * scale)
        total = jnp.sum(old, 1, keepdims=True) + jnp.sum(new, 1, keepdims=True)
        mixed = jnp.dot(
            old.astype(bf16), keys[:held, :kv_width], preferred_element_type=f32
        ) + jnp.dot(new.astype(bf16), keys[held:, :kv_width], preferred_element_type=f32)
        summed = jnp.dot(mixed.astype(bf16), lift, preferred_element_type=f32)
        if not merged:
            live_rows = lax.broadcasted_iota(jnp.int32, (group, 1), 0) < live
            outs[0][...] = jnp.where(live_rows, summed[:, NOPE:] / total, 0.0).astype(bf16)
        elif k == 0:
            outs[0][:, :NOPE] = summed[:, NOPE:]
            outs[0][:, NOPE : NOPE + 1] = peak
            outs[0][:, NOPE + 1 : NOPE + 2] = total
        else:
            outs[k][:, :VDIM] = summed[:, NOPE:].astype(bf16)
            for i, part in enumerate(split3(peak) + split3(total)):
                outs[k][:, VDIM + i : VDIM + i + 1] = part


def merge_kernel(live_ref, own_ref, *refs):
    out_ref = refs[-1]
    live = live_ref[lax.axis_index("row")]
    scale = 1.0 / math.sqrt(NOPE + ROPE)
    parts = [(own_ref[:, :VDIM], own_ref[:, VDIM : VDIM + 1], own_ref[:, VDIM + 1 : VDIM + 2])]
    for ref in refs[:-1]:
        lanes = [ref[:, VDIM + i : VDIM + i + 1].astype(f32) for i in range(6)]
        parts.append(
            (
                ref[:, :VDIM].astype(f32),
                lanes[0] + lanes[1] + lanes[2],
                lanes[3] + lanes[4] + lanes[5],
            )
        )
    peak = functools.reduce(jnp.maximum, [p[1] for p in parts])
    total = 0.0
    summed = 0.0
    for part in parts:
        factor = jnp.exp((part[1] - peak) * scale)
        total += part[2] * factor
        summed += part[0] * factor
    rows = lax.broadcasted_iota(jnp.int32, total.shape, 0)
    out_ref[...] = jnp.where(rows < live, summed / total, 0.0).astype(bf16)


def out_kernel(half, width, *refs):
    mine_ref, other_ref = refs[-2:]
    core = lax.axis_index("col") & 1
    total = 0.0
    for k in range(half):
        total += jnp.dot(refs[k][...], refs[half + k][...], preferred_element_type=f32)
    low, high = total[:, :width], total[:, width:]
    mine_ref[...] = jnp.where(core == 0, low, high)
    other_ref[...] = jnp.where(core == 0, high, low).astype(bf16)


def body(
    tokens, w_down, q_gain, kv_gain, w_q_up, w_kv_up, w_out, latent_cache,
    cache_len, new_len, page_table, home_slot,
):
    count = lax.axis_size("col")
    rows = lax.axis_size("row")
    column = lax.axis_index("col")
    row = lax.axis_index("row")
    group = tokens.shape[0]
    own = group // count
    q_width, kv_width, wide = q_gain.shape[0], kv_gain.shape[0], w_down.shape[1]
    span = min(SPAN, count)
    half = count // 2
    cols = w_out.shape[1] // count
    slot = home_slot[row]

    def swap(value, d):
        return lax.ppermute(value, "col", [(s, s ^ d) for s in range(count)])

    held = latent_cache[0]
    cache = held
    for d in range(1, rows):
        moved = lax.ppermute(held, "row", [(s, (s + d) % rows) for s in range(rows)])
        cache = jnp.where((row + rows - d) % rows == slot, moved, cache)

    def chip_columns(chip):
        return lax.dynamic_slice_in_dim(w_out, chip * 2 * cols, 2 * cols, 1)

    out_weights = [chip_columns(column // 2)] + [
        swap(chip_columns((column ^ d) // 2), d) for d in range(2, count, 2)
    ]
    query_weights = [w_q_up] + [swap(w_q_up, d) for d in range(span, count, span)]
    cosine, sine = angle_tables(cache_len[slot] + jnp.arange(group, dtype=jnp.int32), ROPE)

    even, odd = pl.pallas_call(
        functools.partial(down_kernel, count, own),
        out_shape=[jax.ShapeDtypeStruct((half, own, wide), bf16)] * 2,
        in_specs=[VMEM] * 2,
        out_specs=[VMEM] * 2,
        scratch_shapes=[pltpu.VMEM((group, wide), f32)],
        compiler_params=PARAMS,
        cost_estimate=cost(2 * group * tokens.shape[1] * wide, 2_000_000),
        name="down",
    )(tokens, w_down)
    paired = (even.astype(f32) + swap(odd, 1).astype(f32)).astype(bf16)
    partial = [paired[0]] + [swap(paired[k], 2 * k) for k in range(1, half)]
    block = pl.pallas_call(
        functools.partial(norm_kernel, own, q_width, kv_width),
        out_shape=jax.ShapeDtypeStruct((own, wide), bf16),
        in_specs=[VMEM] * (4 + half),
        out_specs=VMEM,
        compiler_params=PARAMS,
        cost_estimate=cost(1_000_000, 500_000),
        name="norm",
    )(cosine, sine, q_gain[None], kv_gain[None], *partial)

    blocks = [None] * count
    for d in range(0, count, 2):
        blocks[d] = swap(block, d) if d else block
        blocks[d + 1] = swap(blocks[d], 1)
    pieces = [None] * span
    for d in range(0, span, 2):
        pieces[d] = swap(cache, d) if d else cache
        pieces[d + 1] = swap(pieces[d], 1)

    merged = span < count
    heads = count // span
    if merged:
        shapes = [jax.ShapeDtypeStruct((group, 128), f32)] + [
            jax.ShapeDtypeStruct((group, 128), bf16)
        ] * (heads - 1)
    else:
        shapes = [jax.ShapeDtypeStruct((group, VDIM), bf16)]
    keys = span * (cache.shape[0] + own)
    states = pl.pallas_call(
        functools.partial(attend_kernel, span, count, own, q_width, kv_width, merged),
        out_shape=shapes,
        in_specs=[SMEM] * 4 + [VMEM] * (3 + heads + count + span),
        out_specs=[VMEM] * len(shapes),
        scratch_shapes=[
            pltpu.VMEM((group, q_width), f32),
            pltpu.VMEM((span * own, kv_width + ROPE), f32),
            pltpu.VMEM((keys, kv_width + ROPE), bf16),
            pltpu.VMEM((1, span * cache.shape[0]), f32),
        ],
        compiler_params=PARAMS,
        cost_estimate=cost(heads * 4 * group * keys * 300, 3_000_000, heads * group * keys),
        name="attend",
    )(
        home_slot, cache_len, new_len, page_table, cosine, sine, w_kv_up,
        *query_weights, *blocks, *pieces,
    )
    if merged:
        received = [swap(states[k], k * span) for k in range(1, heads)]
        attended = pl.pallas_call(
            merge_kernel,
            out_shape=jax.ShapeDtypeStruct((group, VDIM), bf16),
            in_specs=[SMEM] + [VMEM] * heads,
            out_specs=VMEM,
            compiler_params=PARAMS,
            cost_estimate=cost(1_000_000, 500_000),
            name="merge",
        )(new_len, states[0], *received)
    else:
        attended = states[0]
    gathered = [attended] + [swap(attended, d) for d in range(2, count, 2)]
    mine, other = pl.pallas_call(
        functools.partial(out_kernel, half, cols),
        out_shape=[
            jax.ShapeDtypeStruct((group, cols), f32),
            jax.ShapeDtypeStruct((group, cols), bf16),
        ],
        in_specs=[VMEM] * (2 * half),
        out_specs=[VMEM] * 2,
        compiler_params=PARAMS,
        cost_estimate=cost(2 * group * half * VDIM * 2 * cols, 1_000_000),
        name="out",
    )(*gathered, *out_weights)
    return (mine + swap(other, 1).astype(f32)).astype(bf16)


def solution(mesh):
    return jax.shard_map(
        body,
        mesh=mesh,
        in_specs=(
            P("row", "col"),
            P("col", None),
            P(),
            P(),
            P(None, "col"),
            P(),
            P("col", None),
            P("row", "col", None),
            P(),
            P(),
            P(),
            P(),
        ),
        out_specs=P("row", "col"),
        check_vma=False,
    )
```

```python
import functools
import math

import jax
import jax.numpy as jnp
from jax import lax
from jax.experimental import pallas as pl
from jax.experimental.pallas import tpu as pltpu
from jax.sharding import PartitionSpec as P

NOPE = 64
ROPE = 32
VDIM = 64
HEAD = NOPE + VDIM
SPAN = 4
epsilon = 1e-05
MASKED = -1e30
FLOOR = -1e29

bf16 = jnp.bfloat16
f32 = jnp.float32
VMEM = pl.BlockSpec(memory_space=pltpu.VMEM)
SMEM = pl.BlockSpec(memory_space=pltpu.SMEM)
PARAMS = pltpu.CompilerParams(vmem_limit_bytes=32 * 1024 * 1024)


def cost(flops, moved, special=0):
    return pl.CostEstimate(flops=flops, bytes_accessed=moved, transcendentals=special)


def rotate(values, cosine, sine, axis):
    half = ROPE // 2
    first = lax.slice_in_dim(values, 0, half, axis=axis)
    second = lax.slice_in_dim(values, half, 2 * half, axis=axis)
    return jnp.concatenate(
        [first * cosine - second * sine, second * cosine + first * sine], axis=axis
    )


def down_kernel(count, own, tokens_ref, w_ref, even_ref, odd_ref, sums):
    column = lax.axis_index("col")
    sums[...] = lax.dot_general(
        tokens_ref[...], w_ref[...], (((0,), (0,)), ((), ())), preferred_element_type=f32
    )
    for j in range(count):
        start = pl.multiple_of((column ^ j) * own, own)
        target = odd_ref if j % 2 else even_ref
        target[j // 2] = sums[pl.ds(start, own), :].astype(bf16)


def prepare_kernel(
    span, count, own, page, home_ref, cached_ref, live_ref, page_ref, w_out_ref,
    own_cos, own_sin, cosine, sine, limits, fresh_limits, alive, choice, *refs,
):
    columns, logical = refs[:-1], refs[-1]
    column = lax.axis_index("col")
    row = lax.axis_index("row")
    slot = home_ref[row]
    live = live_ref[row]
    cached = cached_ref[slot]
    rows = choice.shape[0]
    group = count * own
    half = ROPE // 2
    rate = -2.0 * math.log(10000.0) / ROPE

    place = cached + column * own + lax.broadcasted_iota(jnp.int32, (own, half), 0)
    step = lax.broadcasted_iota(jnp.int32, (own, half), 1).astype(f32)
    angle = place.astype(f32) * jnp.exp(step * rate)
    own_cos[...] = jnp.cos(angle)
    own_sin[...] = jnp.sin(angle)
    place = cached + lax.broadcasted_iota(jnp.int32, (half, group), 1)
    step = lax.broadcasted_iota(jnp.int32, (half, group), 0).astype(f32)
    angle = place.astype(f32) * jnp.exp(step * rate)
    cosine[...] = jnp.cos(angle)
    sine[...] = jnp.sin(angle)

    for l in range(page_ref.shape[1]):
        logical[page_ref[slot, l]] = l
    per_piece = limits.shape[0] // span // page
    offset = lax.broadcasted_iota(jnp.int32, (page, 128), 0)
    for j in range(span):
        for p in range(per_piece):
            seen = offset < cached - logical[(column ^ j) * per_piece + p] * page
            start = (j * per_piece + p) * page
            limits[start : start + page, :] = jnp.where(seen, 0.0, MASKED)
    query_id = lax.broadcasted_iota(jnp.int32, (own, group), 1)
    offset = lax.broadcasted_iota(jnp.int32, (own, group), 0)
    for j in range(span):
        fresh_id = (column ^ j) * own + offset
        seen = (fresh_id <= query_id) & (fresh_id < live)
        fresh_limits[j * own : (j + 1) * own, :] = jnp.where(seen, 0.0, MASKED)
    token = lax.broadcasted_iota(jnp.int32, (1, group), 1)
    alive[...] = jnp.where(token < live, 1.0, 0.0)
    source = lax.broadcasted_iota(jnp.int32, choice.shape, 0)
    source = jnp.where(row >= source, row - source, row - source + rows)
    choice[...] = jnp.where(source == slot, 1.0, 0.0)

    width = columns[0].shape[1]
    for i, ref in enumerate(columns):
        start = ((column // 2) ^ i) * width
        if width % 128 == 0:
            ref[...] = w_out_ref[:, pl.ds(pl.multiple_of(start, 128), width)]
        else:
            taken = w_out_ref[:, :width]
            for chip in range(1, count // 2):
                taken = jnp.where(
                    (column // 2) ^ i == chip, w_out_ref[:, chip * width : (chip + 1) * width], taken
                )
            ref[...] = taken


def norm_kernel(q_width, kv_width, cos_ref, sin_ref, q_gain_ref, kv_gain_ref, *refs):
    out_ref = refs[-1]
    total = refs[0][...].astype(f32)
    for ref in refs[1:-1]:
        total += ref[...].astype(f32)

    def scaled(values, gain):
        mean = jnp.mean(values * values, axis=-1, keepdims=True)
        return values * lax.rsqrt(mean + epsilon) * gain

    out_ref[:, :q_width] = scaled(total[:, :q_width], q_gain_ref[...]).astype(bf16)
    out_ref[:, q_width : q_width + kv_width] = scaled(
        total[:, q_width : q_width + kv_width], kv_gain_ref[...]
    ).astype(bf16)
    out_ref[:, q_width + kv_width :] = rotate(
        total[:, q_width + kv_width :], cos_ref[...], sin_ref[...], 1
    ).astype(bf16)


def split3(value):
    high = value.astype(bf16).astype(f32)
    middle = (value - high).astype(bf16).astype(f32)
    return [high, middle, value - high - middle]


def attend_kernel(span, count, own, q_width, kv_width, cos_ref, sin_ref, limits, fresh_limits, w_kv_ref, *refs):
    heads = count // span
    weights, refs = refs[:heads], refs[heads:]
    blocks, refs = refs[:count], refs[count:]
    pieces, (out_ref, query_rows, fresh, keys) = refs[:span], refs[span:]
    column = lax.axis_index("col")
    group = count * own
    piece = pieces[0].shape[1]
    held = span * piece
    for j in range(count):
        start = pl.multiple_of((column ^ j) * own, own)
        query_rows[pl.ds(start, own), :] = blocks[j][:, :q_width].astype(f32)
        if j < span:
            fresh[j * own : (j + 1) * own, :] = blocks[j][:, q_width:].astype(f32)
    for j in range(span):
        keys[:, j * piece : (j + 1) * piece] = pieces[j][...]
    fresh_keys = fresh[...].astype(bf16)
    latent = query_rows[...].astype(bf16)
    scale = 1.0 / math.sqrt(NOPE + ROPE)
    stats = []
    for k in range(heads):
        head = column ^ (k * span)
        lift = w_kv_ref[:, pl.ds(pl.multiple_of(head * HEAD, HEAD), HEAD)]
        projected = lax.dot_general(
            weights[k][...], latent, (((1,), (1,)), ((), ())), preferred_element_type=f32
        )
        turned = rotate(projected[NOPE:], cos_ref[...], sin_ref[...], 0)
        plain = jnp.dot(
            lift[:, :NOPE], projected[:NOPE].astype(bf16), preferred_element_type=f32
        )
        query = jnp.concatenate([plain.astype(bf16), turned.astype(bf16)], axis=0)
        old = lax.dot_general(
            keys[...], query, (((0,), (0,)), ((), ())), preferred_element_type=f32
        )
        old += jnp.concatenate([limits[...]] * (group // 128), axis=1)
        new = jnp.dot(fresh_keys, query, preferred_element_type=f32) + fresh_limits[...]
        peak = jnp.maximum(jnp.max(old, 0, keepdims=True), jnp.max(new, 0, keepdims=True))
        peak = jnp.maximum(peak, FLOOR)
        old = jnp.exp((old - peak) * scale)
        new = jnp.exp((new - peak) * scale)
        total = jnp.sum(old, 0, keepdims=True) + jnp.sum(new, 0, keepdims=True)
        mixed = jnp.dot(
            keys[:kv_width, :], old.astype(bf16), preferred_element_type=f32
        ) + lax.dot_general(
            fresh_keys[:, :kv_width], new.astype(bf16),
            (((0,), (0,)), ((), ())), preferred_element_type=f32,
        )
        summed = lax.dot_general(
            lift, mixed.astype(bf16), (((0,), (0,)), ((), ())), preferred_element_type=f32
        )
        out_ref[k * VDIM : (k + 1) * VDIM, :] = summed[NOPE:].astype(bf16)
        stats += split3(peak) + split3(total) + [jnp.zeros_like(total)] * 2
    out_ref[heads * VDIM :, :] = jnp.concatenate(stats, axis=0).astype(bf16)


def out_kernel(span, count, width, alive_ref, *refs):
    half = count // 2
    heads = count // span
    columns, refs = refs[:half], refs[half:]
    states, (mine_ref, other_ref, attended, weights) = refs[:half], refs[half:]
    scale = 1.0 / math.sqrt(NOPE + ROPE)
    for i in range(half):
        weights[i * VDIM : (i + 1) * VDIM, :] = columns[i][...]
        parts = []
        for k in range(heads):
            ref = states[i ^ (k * span // 2)]
            lanes = ref[heads * VDIM :, :].astype(f32)[8 * k : 8 * k + 6]
            parts.append(
                (
                    ref[k * VDIM : (k + 1) * VDIM, :].astype(f32),
                    lanes[0:1] + lanes[1:2] + lanes[2:3],
                    lanes[3:4] + lanes[4:5] + lanes[5:6],
                )
            )
        peak = functools.reduce(jnp.maximum, [p[1] for p in parts])
        total = 0.0
        summed = 0.0
        for part in parts:
            factor = jnp.exp((part[1] - peak) * scale)
            total += part[2] * factor
            summed += part[0] * factor
        factor = jnp.where(alive_ref[...] > 0, 1.0 / total, 0.0)
        attended[i * VDIM : (i + 1) * VDIM, :] = (summed * factor).astype(bf16)
    product = lax.dot_general(
        weights[...], attended[...], (((0,), (0,)), ((), ())), preferred_element_type=f32
    )
    low, high = product[:width], product[width:]
    core = lax.axis_index("col") & 1
    mine_ref[...] = jnp.where(core == 0, low, high)
    other_ref[...] = jnp.where(core == 0, high, low).astype(bf16)


def body(
    tokens, w_down, q_gain, kv_gain, w_q_up, w_kv_up, w_out, latent_cache,
    cache_len, new_len, page_table, home_slot,
):
    count = lax.axis_size("col")
    rows = lax.axis_size("row")
    group = tokens.shape[0]
    own = group // count
    q_width, kv_width, wide = q_gain.shape[0], kv_gain.shape[0], w_down.shape[1]
    span = min(SPAN, count)
    half = count // 2
    heads = count // span
    cols = w_out.shape[1] // count
    piece = latent_cache.shape[1]
    page = piece * count // page_table.shape[1]

    def swap(value, d):
        return lax.ppermute(value, "col", [(s, s ^ d) for s in range(count)])

    def call(kernel, name, shapes, operands, scratch=(), scalars=0):
        single = not isinstance(shapes, list)
        return pl.pallas_call(
            kernel,
            out_shape=shapes,
            in_specs=[SMEM] * scalars + [VMEM] * (len(operands) - scalars),
            out_specs=VMEM if single else [VMEM] * len(shapes),
            scratch_shapes=list(scratch),
            compiler_params=PARAMS,
            cost_estimate=cost(1000, 1000),
            name=name,
        )(*operands)

    shape = jax.ShapeDtypeStruct
    held = latent_cache[0].T
    moved = [
        lax.ppermute(held, "row", [(s, (s + d) % rows) for s in range(rows)])
        for d in range(1, rows)
    ]
    query_weights = [w_q_up.T] + [swap(w_q_up.T, d) for d in range(span, count, span)]
    even, odd = call(
        functools.partial(down_kernel, count, own), "down",
        [shape((half, own, wide), bf16)] * 2, (tokens.T, w_down),
        [pltpu.VMEM((group, wide), f32)],
    )
    paired = (even.astype(f32) + swap(odd, 1).astype(f32)).astype(bf16)
    paired, w_out, home_slot = lax.optimization_barrier((paired, w_out, home_slot))
    partial = [paired[0]] + [swap(paired[k], 2 * k) for k in range(1, half)]
    own_cos, own_sin, cosine, sine, limits, fresh_limits, alive, choice, *columns = call(
        functools.partial(prepare_kernel, span, count, own, page), "prepare",
        [shape((own, ROPE // 2), f32)] * 2
        + [shape((ROPE // 2, group), f32)] * 2
        + [shape((span * piece, 128), f32), shape((span * own, group), f32)]
        + [shape((1, group), f32), shape((rows, group), f32)]
        + [shape((w_out.shape[0], 2 * cols), bf16)] * half,
        (home_slot, cache_len, new_len, page_table, w_out),
        [pltpu.SMEM((page_table.shape[1],), jnp.int32)], 4,
    )
    columns = columns[:1] + [swap(columns[i], 2 * i) for i in range(1, half)]
    block = call(
        functools.partial(norm_kernel, q_width, kv_width), "norm", shape((own, wide), bf16),
        (own_cos, own_sin, q_gain[None], kv_gain[None], *partial),
    )
    block, *moved = lax.optimization_barrier((block, *moved))
    cache = held
    for d in range(1, rows):
        cache = jnp.where(choice[d, :piece] > 0, moved[d - 1], cache)
    blocks = [None] * count
    for d in range(0, count, 2):
        blocks[d] = swap(block, d) if d else block
        blocks[d + 1] = swap(blocks[d], 1)
    pieces = [None] * span
    for d in range(0, span, 2):
        pieces[d] = swap(cache, d) if d else cache
        pieces[d + 1] = swap(pieces[d], 1)
    state = call(
        functools.partial(attend_kernel, span, count, own, q_width, kv_width), "attend",
        shape((heads * (VDIM + 8), group), bf16),
        (cosine, sine, limits, fresh_limits, w_kv_up, *query_weights, *blocks, *pieces),
        [
            pltpu.VMEM((group, q_width), f32),
            pltpu.VMEM((span * own, kv_width + ROPE), f32),
            pltpu.VMEM((kv_width + ROPE, span * piece), bf16),
        ],
    )
    states = [state] + [swap(state, d) for d in range(2, count, 2)]
    mine, other = call(
        functools.partial(out_kernel, span, count, cols), "out",
        [shape((cols, group), f32), shape((cols, group), bf16)],
        (alive, *columns, *states),
        [
            pltpu.VMEM((half * VDIM, group), bf16),
            pltpu.VMEM((half * VDIM, 2 * cols), bf16),
        ],
    )
    return (mine + swap(other, 1).astype(f32)).astype(bf16).T


def solution(mesh):
    return jax.shard_map(
        body,
        mesh=mesh,
        in_specs=(
            P("row", "col"),
            P("col", None),
            P(),
            P(),
            P(None, "col"),
            P(),
            P("col", None),
            P("row", "col", None),
            P(),
            P(),
            P(),
            P(),
        ),
        out_specs=P("row", "col"),
        check_vma=False,
    )
```

```python
import functools
import math

import jax
import jax.numpy as jnp
from jax import lax
from jax.experimental import pallas as pl
from jax.experimental.pallas import tpu as pltpu
from jax.sharding import PartitionSpec as P

NOPE = 64
ROPE = 32
VDIM = 64
HEAD = NOPE + VDIM
SPAN = 4
EXTRA = 16
epsilon = 1e-05
MASKED = -1e30
FLOOR = -1e29

bf16 = jnp.bfloat16
f32 = jnp.float32
VMEM = pl.BlockSpec(memory_space=pltpu.VMEM)
SMEM = pl.BlockSpec(memory_space=pltpu.SMEM)
PARAMS = pltpu.CompilerParams(vmem_limit_bytes=32 * 1024 * 1024)


def cost(flops, moved, special=0):
    return pl.CostEstimate(flops=flops, bytes_accessed=moved, transcendentals=special)


def padded(lanes):
    return -(-lanes // 128) * 128


def rotate(values, cosine, sine, axis):
    half = ROPE // 2
    first = lax.slice_in_dim(values, 0, half, axis=axis)
    second = lax.slice_in_dim(values, half, 2 * half, axis=axis)
    return jnp.concatenate(
        [first * cosine - second * sine, second * cosine + first * sine], axis=axis
    )


def down_kernel(count, own, tokens_ref, w_ref, even_ref, odd_ref, sums):
    column = lax.axis_index("col")
    sums[...] = lax.dot_general(
        tokens_ref[...], w_ref[...], (((0,), (0,)), ((), ())), preferred_element_type=f32
    )
    for j in range(count):
        start = pl.multiple_of((column ^ j) * own, own)
        target = odd_ref if j % 2 else even_ref
        target[j // 2] = sums[pl.ds(start, own), :].astype(bf16)


def prepare_kernel(
    span, count, own, page, home_ref, cached_ref, live_ref, page_ref, q_gain_ref, kv_gain_ref,
    own_cos, own_sin, cosine, sine, limits, fresh_limits, alive, choice, q_gain, kv_gain, logical,
):
    q_gain[...] = q_gain_ref[...]
    kv_gain[...] = kv_gain_ref[...]
    column = lax.axis_index("col")
    row = lax.axis_index("row")
    slot = home_ref[row]
    live = live_ref[row]
    cached = cached_ref[slot]
    rows = choice.shape[0]
    group = count * own
    half = ROPE // 2
    rate = -2.0 * math.log(10000.0) / ROPE

    place = cached + column * own + lax.broadcasted_iota(jnp.int32, (own, half), 0)
    step = lax.broadcasted_iota(jnp.int32, (own, half), 1).astype(f32)
    angle = place.astype(f32) * jnp.exp(step * rate)
    own_cos[...] = jnp.cos(angle)
    own_sin[...] = jnp.sin(angle)
    place = cached + lax.broadcasted_iota(jnp.int32, (half, group), 1)
    step = lax.broadcasted_iota(jnp.int32, (half, group), 0).astype(f32)
    angle = place.astype(f32) * jnp.exp(step * rate)
    cosine[...] = jnp.cos(angle)
    sine[...] = jnp.sin(angle)

    for l in range(page_ref.shape[1]):
        logical[page_ref[slot, l]] = l
    per_piece = limits.shape[1] // span // page
    offset = lax.broadcasted_iota(jnp.int32, (EXTRA, page), 1)
    line = lax.broadcasted_iota(jnp.int32, (EXTRA, page), 0)
    for j in range(span):
        for p in range(per_piece):
            seen = offset < cached - logical[(column ^ j) * per_piece + p] * page
            start = (j * per_piece + p) * page
            limits[:, start : start + page] = jnp.where(seen | (line > 0), 0.0, MASKED).astype(bf16)
    query_id = lax.broadcasted_iota(jnp.int32, (own, group), 1)
    offset = lax.broadcasted_iota(jnp.int32, (own, group), 0)
    for j in range(span):
        fresh_id = (column ^ j) * own + offset
        seen = (fresh_id <= query_id) & (fresh_id < live)
        fresh_limits[j * own : (j + 1) * own, :] = jnp.where(seen, 0.0, MASKED)
    token = lax.broadcasted_iota(jnp.int32, (1, group), 1)
    alive[...] = jnp.where(token < live, 1.0, 0.0)
    source = lax.broadcasted_iota(jnp.int32, choice.shape, 0)
    source = jnp.where(row >= source, row - source, row - source + rows)
    choice[...] = jnp.where(source == slot, 1.0, 0.0)


def sum_kernel(count, wide, even_ref, odd_ref, w_out_ref, *outs):
    half = count // 2
    own = even_ref.shape[1]
    width = 2 * (w_out_ref.shape[1] // count)
    chip = lax.axis_index("col") // 2
    for i, ref in enumerate(outs):
        ref[:, :wide] = (even_ref[i].astype(f32) + odd_ref[i].astype(f32)).astype(bf16)
        start = (chip ^ i) * width
        if width % 128 == 0:
            taken = w_out_ref[:, pl.ds(pl.multiple_of(start, 128), width)]
        else:
            taken = w_out_ref[:, :width]
            for k in range(1, half):
                taken = jnp.where(chip ^ i == k, w_out_ref[:, k * width : (k + 1) * width], taken)
        for p in range(taken.shape[0] // own):
            lane = padded(wide) + p * padded(width)
            ref[:, lane : lane + width] = taken[p * own : (p + 1) * own]


def norm_kernel(q_width, kv_width, cos_ref, sin_ref, q_gain_ref, kv_gain_ref, *refs):
    out_ref = refs[-1]
    wide = out_ref.shape[1]
    total = refs[0][:, :wide].astype(f32)
    for ref in refs[1:-1]:
        total += ref[:, :wide].astype(f32)

    def scaled(values, gain):
        mean = jnp.mean(values * values, axis=-1, keepdims=True)
        return values * lax.rsqrt(mean + epsilon) * gain

    out_ref[:, :q_width] = scaled(total[:, :q_width], q_gain_ref[...]).astype(bf16)
    out_ref[:, q_width : q_width + kv_width] = scaled(
        total[:, q_width : q_width + kv_width], kv_gain_ref[...]
    ).astype(bf16)
    out_ref[:, q_width + kv_width :] = rotate(
        total[:, q_width + kv_width :], cos_ref[...], sin_ref[...], 1
    ).astype(bf16)


def split3(value):
    high = value.astype(bf16).astype(f32)
    middle = (value - high).astype(bf16).astype(f32)
    return [high, middle, value - high - middle]


def attend_kernel(
    span, count, own, q_width, kv_width, cos_ref, sin_ref, limits, fresh_limits, w_kv_ref, *refs
):
    heads = count // span
    weights, refs = refs[:heads], refs[heads:]
    blocks, refs = refs[:count], refs[count:]
    pieces, (out_ref, query_rows, fresh, keys) = refs[:span], refs[span:]
    column = lax.axis_index("col")
    group = count * own
    piece = pieces[0].shape[1]
    held = span * piece
    for j in range(count):
        start = pl.multiple_of((column ^ j) * own, own)
        query_rows[pl.ds(start, own), :] = blocks[j][:, :q_width].astype(f32)
        if j < span:
            fresh[j * own : (j + 1) * own, :] = blocks[j][:, q_width:].astype(f32)
    for j in range(span):
        keys[: kv_width + ROPE, j * piece : (j + 1) * piece] = pieces[j][...]
    keys[kv_width + ROPE :, :] = limits[...]
    fresh_keys = fresh[...].astype(bf16)
    latent = query_rows[...].astype(bf16)
    scale = 1.0 / math.sqrt(NOPE + ROPE)
    line = lax.broadcasted_iota(jnp.int32, (EXTRA, group), 0)
    first_row = jnp.where(line == 0, 1.0, 0.0).astype(bf16)
    stats = []
    for k in range(heads):
        head = column ^ (k * span)
        lift = w_kv_ref[:, pl.ds(pl.multiple_of(head * HEAD, HEAD), HEAD)]
        projected = lax.dot_general(
            weights[k][...], latent, (((1,), (1,)), ((), ())), preferred_element_type=f32
        )
        turned = rotate(projected[NOPE:], cos_ref[...], sin_ref[...], 0)
        plain = jnp.dot(
            lift[:, :NOPE], projected[:NOPE].astype(bf16), preferred_element_type=f32
        )
        query = jnp.concatenate([plain.astype(bf16), turned.astype(bf16)], axis=0)
        old = lax.dot_general(
            keys[...], jnp.concatenate([query, first_row], axis=0),
            (((0,), (0,)), ((), ())), preferred_element_type=f32,
        )
        new = jnp.dot(fresh_keys, query, preferred_element_type=f32) + fresh_limits[...]
        peak = jnp.maximum(jnp.max(old, 0, keepdims=True), jnp.max(new, 0, keepdims=True))
        peak = jnp.maximum(peak, FLOOR)
        old = jnp.exp((old - peak) * scale)
        new = jnp.exp((new - peak) * scale)
        total = jnp.sum(old, 0, keepdims=True) + jnp.sum(new, 0, keepdims=True)
        mixed = jnp.dot(
            keys[:kv_width, :], old.astype(bf16), preferred_element_type=f32
        ) + lax.dot_general(
            fresh_keys[:, :kv_width], new.astype(bf16),
            (((0,), (0,)), ((), ())), preferred_element_type=f32,
        )
        summed = lax.dot_general(
            lift, mixed.astype(bf16), (((0,), (0,)), ((), ())), preferred_element_type=f32
        )
        out_ref[k * VDIM : (k + 1) * VDIM, :] = summed[NOPE:].astype(bf16)
        stats += split3(peak) + split3(total) + [jnp.zeros_like(total)] * 2
    out_ref[heads * VDIM :, :] = jnp.concatenate(stats, axis=0).astype(bf16)


def out_kernel(span, count, width, wide, alive_ref, *refs):
    half = count // 2
    heads = count // span
    columns, refs = refs[:half], refs[half:]
    states, (mine_ref, other_ref, attended, weights) = refs[:half], refs[half:]
    scale = 1.0 / math.sqrt(NOPE + ROPE)
    for i in range(half):
        own = columns[i].shape[0]
        for p in range(VDIM // own):
            lane = padded(wide) + p * padded(2 * width)
            row = i * VDIM + p * own
            weights[row : row + own, :] = columns[i][:, lane : lane + 2 * width].astype(f32)
        parts = []
        for k in range(heads):
            ref = states[i ^ (k * span // 2)]
            lanes = ref[heads * VDIM :, :].astype(f32)[8 * k : 8 * k + 6]
            parts.append(
                (
                    ref[k * VDIM : (k + 1) * VDIM, :].astype(f32),
                    lanes[0:1] + lanes[1:2] + lanes[2:3],
                    lanes[3:4] + lanes[4:5] + lanes[5:6],
                )
            )
        peak = functools.reduce(jnp.maximum, [p[1] for p in parts])
        total = 0.0
        summed = 0.0
        for part in parts:
            factor = jnp.exp((part[1] - peak) * scale)
            total += part[2] * factor
            summed += part[0] * factor
        factor = jnp.where(alive_ref[...] > 0, 1.0 / total, 0.0)
        attended[i * VDIM : (i + 1) * VDIM, :] = (summed * factor).astype(bf16)
    product = lax.dot_general(
        weights[...].astype(bf16), attended[...], (((0,), (0,)), ((), ())), preferred_element_type=f32
    )
    low, high = product[:width], product[width:]
    core = lax.axis_index("col") & 1
    mine_ref[...] = jnp.where(core == 0, low, high)
    other_ref[...] = jnp.where(core == 0, high, low).astype(bf16)


def body(
    tokens, w_down, q_gain, kv_gain, w_q_up, w_kv_up, w_out, latent_cache,
    cache_len, new_len, page_table, home_slot,
):
    count = lax.axis_size("col")
    rows = lax.axis_size("row")
    group = tokens.shape[0]
    own = group // count
    q_width, kv_width, wide = q_gain.shape[0], kv_gain.shape[0], w_down.shape[1]
    span = min(SPAN, count)
    half = count // 2
    heads = count // span
    cols = w_out.shape[1] // count
    piece = latent_cache.shape[1]
    page = piece * count // page_table.shape[1]

    def swap(value, d):
        return lax.ppermute(value, "col", [(s, s ^ d) for s in range(count)])

    def call(kernel, name, shapes, operands, scratch=(), scalars=0):
        single = not isinstance(shapes, list)
        result = pl.pallas_call(
            kernel,
            out_shape=shapes,
            in_specs=[SMEM] * scalars + [VMEM] * (len(operands) - scalars),
            out_specs=VMEM if single else [VMEM] * len(shapes),
            scratch_shapes=list(scratch),
            compiler_params=PARAMS,
            cost_estimate=cost(1000, 1000),
            name=name,
        )(*operands)
        return result if single else list(result)

    shape = jax.ShapeDtypeStruct
    held = latent_cache[0].T
    moved = [
        lax.ppermute(held, "row", [(s, (s + d) % rows) for s in range(rows)])
        for d in range(1, rows)
    ]
    query_weights = [w_q_up.T] + [swap(w_q_up.T, d) for d in range(span, count, span)]
    even, odd = call(
        functools.partial(down_kernel, count, own), "down",
        [shape((half, own, wide), bf16)] * 2, (tokens.T, w_down),
        [pltpu.VMEM((group, wide), f32)],
    )
    length = padded(wide) + VDIM // own * padded(2 * cols)
    paired = call(
        functools.partial(sum_kernel, count, wide), "sum",
        [shape((own, length), bf16)] * half, (even, swap(odd, 1), w_out),
    )
    paired[0], home_slot = lax.optimization_barrier((paired[0], home_slot))
    partial = [paired[0]] + [swap(paired[k], 2 * k) for k in range(1, half)]
    own_cos, own_sin, cosine, sine, limits, fresh_limits, alive, choice, q_scale, kv_scale = call(
        functools.partial(prepare_kernel, span, count, own, page), "prepare",
        [shape((own, ROPE // 2), f32)] * 2
        + [shape((ROPE // 2, group), f32)] * 2
        + [shape((EXTRA, span * piece), bf16), shape((span * own, group), f32)]
        + [shape((1, group), f32), shape((rows, group), f32)]
        + [shape((1, q_width), f32), shape((1, kv_width), f32)],
        (home_slot, cache_len, new_len, page_table, q_gain[None], kv_gain[None]),
        [pltpu.SMEM((page_table.shape[1],), jnp.int32)], 4,
    )
    block = call(
        functools.partial(norm_kernel, q_width, kv_width), "norm", shape((own, wide), bf16),
        (own_cos, own_sin, q_scale, kv_scale, *partial),
    )
    blocks = [None] * count
    for d in range(0, count, 2):
        blocks[d] = swap(block, d) if d else block
    block, moved[-1] = lax.optimization_barrier((block, moved[-1]))
    tied = lax.optimization_barrier((*blocks[2::2], *moved[:-1]))
    blocks[2::2], moved[:-1] = tied[: half - 1], tied[half - 1 :]
    cache = held
    for d in range(1, rows):
        cache = jnp.where(choice[d, :piece] > 0, moved[d - 1], cache)
    for d in range(0, count, 2):
        blocks[d + 1] = swap(blocks[d], 1)
    pieces = [None] * span
    for d in range(0, span, 2):
        pieces[d] = swap(cache, d) if d else cache
        pieces[d + 1] = swap(pieces[d], 1)
    state = call(
        functools.partial(attend_kernel, span, count, own, q_width, kv_width), "attend",
        shape((heads * (VDIM + 8), group), bf16),
        (cosine, sine, limits, fresh_limits, w_kv_up, *query_weights, *blocks, *pieces),
        [
            pltpu.VMEM((group, q_width), f32),
            pltpu.VMEM((span * own, kv_width + ROPE), f32),
            pltpu.VMEM((kv_width + ROPE + EXTRA, span * piece), bf16),
        ],
    )
    states = [state] + [swap(state, d) for d in range(2, count, 2)]
    mine, other = call(
        functools.partial(out_kernel, span, count, cols, wide), "out",
        [shape((cols, group), f32), shape((cols, group), bf16)],
        (alive, *partial, *states),
        [
            pltpu.VMEM((half * VDIM, group), bf16),
            pltpu.VMEM((half * VDIM, 2 * cols), f32),
        ],
    )
    return (mine + swap(other, 1).astype(f32)).astype(bf16).T


def solution(mesh):
    return jax.shard_map(
        body,
        mesh=mesh,
        in_specs=(
            P("row", "col"),
            P("col", None),
            P(),
            P(),
            P(None, "col"),
            P(),
            P("col", None),
            P("row", "col", None),
            P(),
            P(),
            P(),
            P(),
        ),
        out_specs=P("row", "col"),
        check_vma=False,
    )
```

```python
import functools
import math

import jax
import jax.numpy as jnp
from jax import lax
from jax.experimental import pallas as pl
from jax.experimental.pallas import tpu as pltpu
from jax.sharding import PartitionSpec as P

NOPE = 64
ROPE = 32
VDIM = 64
HEAD = NOPE + VDIM
SPAN = 4
EXTRA = 16
epsilon = 1e-05
MASKED = -1e30
FLOOR = -1e29

bf16 = jnp.bfloat16
f32 = jnp.float32
VMEM = pl.BlockSpec(memory_space=pltpu.VMEM)
SMEM = pl.BlockSpec(memory_space=pltpu.SMEM)
PARAMS = pltpu.CompilerParams(vmem_limit_bytes=32 * 1024 * 1024)


def cost(flops, moved, special=0):
    return pl.CostEstimate(flops=flops, bytes_accessed=moved, transcendentals=special)


def padded(lanes):
    return -(-lanes // 128) * 128


def rotate(values, cosine, sine, axis):
    half = ROPE // 2
    first = lax.slice_in_dim(values, 0, half, axis=axis)
    second = lax.slice_in_dim(values, half, 2 * half, axis=axis)
    return jnp.concatenate(
        [first * cosine - second * sine, second * cosine + first * sine], axis=axis
    )


def down_kernel(count, own, tokens_ref, w_ref, even_ref, odd_ref, sums):
    column = lax.axis_index("col")
    sums[...] = lax.dot_general(
        tokens_ref[...], w_ref[...], (((0,), (0,)), ((), ())), preferred_element_type=f32
    )
    for j in range(count):
        start = pl.multiple_of((column ^ j) * own, own)
        target = odd_ref if j % 2 else even_ref
        target[j // 2] = sums[pl.ds(start, own), :].astype(bf16)


def prepare_kernel(
    span, count, own, page, home_ref, cached_ref, live_ref, page_ref, q_gain_ref, kv_gain_ref,
    own_cos, own_sin, cosine, sine, limits, fresh_limits, alive, choice, q_gain, kv_gain, logical,
):
    q_gain[...] = q_gain_ref[...]
    kv_gain[...] = kv_gain_ref[...]
    column = lax.axis_index("col")
    row = lax.axis_index("row")
    slot = home_ref[row]
    live = live_ref[row]
    cached = cached_ref[slot]
    rows = choice.shape[0]
    group = count * own
    half = ROPE // 2
    rate = -2.0 * math.log(10000.0) / ROPE

    place = cached + column * own + lax.broadcasted_iota(jnp.int32, (own, half), 0)
    step = lax.broadcasted_iota(jnp.int32, (own, half), 1).astype(f32)
    angle = place.astype(f32) * jnp.exp(step * rate)
    own_cos[...] = jnp.cos(angle)
    own_sin[...] = jnp.sin(angle)
    place = cached + lax.broadcasted_iota(jnp.int32, (half, group), 1)
    step = lax.broadcasted_iota(jnp.int32, (half, group), 0).astype(f32)
    angle = place.astype(f32) * jnp.exp(step * rate)
    cosine[...] = jnp.cos(angle)
    sine[...] = jnp.sin(angle)

    for l in range(page_ref.shape[1]):
        logical[page_ref[slot, l]] = l
    per_piece = limits.shape[1] // span // page
    offset = lax.broadcasted_iota(jnp.int32, (EXTRA, page), 1)
    line = lax.broadcasted_iota(jnp.int32, (EXTRA, page), 0)
    for j in range(span):
        for p in range(per_piece):
            seen = offset < cached - logical[(column ^ j) * per_piece + p] * page
            start = (j * per_piece + p) * page
            limits[:, start : start + page] = jnp.where(seen | (line > 0), 0.0, MASKED).astype(bf16)
    query_id = lax.broadcasted_iota(jnp.int32, (own, group), 1)
    offset = lax.broadcasted_iota(jnp.int32, (own, group), 0)
    for j in range(span):
        fresh_id = (column ^ j) * own + offset
        seen = (fresh_id <= query_id) & (fresh_id < live)
        fresh_limits[j * own : (j + 1) * own, :] = jnp.where(seen, 0.0, MASKED)
    token = lax.broadcasted_iota(jnp.int32, (1, group), 1)
    alive[...] = jnp.where(token < live, 1.0, 0.0)
    source = lax.broadcasted_iota(jnp.int32, choice.shape, 0)
    source = jnp.where(row >= source, row - source, row - source + rows)
    choice[...] = jnp.where(source == slot, 1.0, 0.0)


def sum_kernel(count, wide, even_ref, odd_ref, w_out_ref, *outs):
    half = count // 2
    own = even_ref.shape[1]
    width = 2 * (w_out_ref.shape[1] // count)
    chip = lax.axis_index("col") // 2
    for i, ref in enumerate(outs):
        ref[:, :wide] = (even_ref[i].astype(f32) + odd_ref[i].astype(f32)).astype(bf16)
        start = (chip ^ i) * width
        if width % 128 == 0:
            taken = w_out_ref[:, pl.ds(pl.multiple_of(start, 128), width)]
        else:
            taken = w_out_ref[:, :width]
            for k in range(1, half):
                taken = jnp.where(chip ^ i == k, w_out_ref[:, k * width : (k + 1) * width], taken)
        for p in range(taken.shape[0] // own):
            lane = padded(wide) + p * padded(width)
            ref[:, lane : lane + width] = taken[p * own : (p + 1) * own]


def norm_kernel(q_width, kv_width, cos_ref, sin_ref, q_gain_ref, kv_gain_ref, *refs):
    out_ref = refs[-1]
    wide = q_width + kv_width + ROPE
    total = refs[0][:, :wide].astype(f32)
    for ref in refs[1:-1]:
        total += ref[:, :wide].astype(f32)

    def scaled(values, gain):
        mean = jnp.mean(values * values, axis=-1, keepdims=True)
        return values * lax.rsqrt(mean + epsilon) * gain

    out_ref[:, :q_width] = scaled(total[:, :q_width], q_gain_ref[...]).astype(bf16)
    out_ref[:, q_width : q_width + kv_width] = scaled(
        total[:, q_width : q_width + kv_width], kv_gain_ref[...]
    ).astype(bf16)
    out_ref[:, q_width + kv_width : wide] = rotate(
        total[:, q_width + kv_width :], cos_ref[...], sin_ref[...], 1
    ).astype(bf16)
    out_ref[:, wide:] = jnp.zeros_like(out_ref[:, wide:])


def split3(value):
    high = value.astype(bf16).astype(f32)
    middle = (value - high).astype(bf16).astype(f32)
    return [high, middle, value - high - middle]


def weigh(query, keys, fresh, fresh_bias, kv_width):
    scale = 1.0 / math.sqrt(NOPE + ROPE)
    scores = [
        lax.dot_general(keys, query, (((0,), (0,)), ((), ())), preferred_element_type=f32)
    ]
    if fresh is not None:
        new = jnp.dot(fresh, query[: fresh.shape[1]], preferred_element_type=f32)
        scores.append(new + jnp.concatenate([fresh_bias] * (new.shape[1] // fresh_bias.shape[1]), 1))
    peak = functools.reduce(jnp.maximum, [jnp.max(s, 0, keepdims=True) for s in scores])
    peak = jnp.maximum(peak, FLOOR)
    weights = [jnp.exp((s - peak) * scale) for s in scores]
    total = sum(jnp.sum(w, 0, keepdims=True) for w in weights)
    mixed = jnp.dot(keys[:kv_width], weights[0].astype(bf16), preferred_element_type=f32)
    if fresh is not None:
        mixed += lax.dot_general(
            fresh[:, :kv_width], weights[1].astype(bf16),
            (((0,), (0,)), ((), ())), preferred_element_type=f32,
        )
    return peak, total, mixed.astype(bf16)


def lifted(w_kv_ref, column, k, span):
    head = column ^ (k * span)
    return w_kv_ref[:, pl.ds(pl.multiple_of(head * HEAD, HEAD), HEAD)]


def begin_kernel(
    span, count, own, q_width, kv_width, cos_ref, sin_ref, limits, fresh_limits, w_kv_ref, *refs
):
    heads = count // span
    weights, refs = refs[:heads], refs[heads:]
    blocks, refs = refs[:count], refs[count:]
    pieces, (query_ref, summed_ref, peak_ref, total_ref, query_rows, fresh, keys) = refs[:2], refs[2:]
    column = lax.axis_index("col")
    group = count * own
    piece = pieces[0].shape[1]
    wide = kv_width + ROPE
    for j in range(count):
        start = pl.multiple_of((column ^ j) * own, own)
        query_rows[pl.ds(start, own), :] = blocks[j][:, :q_width].astype(query_rows.dtype)
        if j < span:
            fresh[j * own : (j + 1) * own, :] = blocks[j][:, q_width : q_width + wide].astype(fresh.dtype)
    for j in range(2):
        keys[:wide, j * piece : (j + 1) * piece] = pieces[j][...]
    keys[wide:, :] = limits[:, : 2 * piece]
    latent = query_rows[...].astype(bf16)
    line = lax.broadcasted_iota(jnp.int32, (EXTRA, group), 0)
    first_row = jnp.where(line == 0, 1.0, 0.0).astype(bf16)
    for k in range(heads):
        projected = lax.dot_general(
            weights[k][...], latent, (((1,), (1,)), ((), ())), preferred_element_type=f32
        )
        turned = rotate(projected[NOPE:], cos_ref[...], sin_ref[...], 0)
        plain = jnp.dot(
            lifted(w_kv_ref, column, k, span)[:, :NOPE],
            projected[:NOPE].astype(bf16), preferred_element_type=f32,
        )
        lanes = slice(k * group, (k + 1) * group)
        query_ref[:kv_width, lanes] = plain.astype(bf16)
        query_ref[kv_width:wide, lanes] = turned.astype(bf16)
        query_ref[wide:, lanes] = first_row
    peak, total, mixed = weigh(
        query_ref[...], keys[...], fresh[...].astype(bf16), fresh_limits[...], kv_width
    )
    peak_ref[...] = peak
    total_ref[...] = total
    for k in range(heads):
        summed = lax.dot_general(
            lifted(w_kv_ref, column, k, span), mixed[:, k * group : (k + 1) * group],
            (((0,), (0,)), ((), ())), preferred_element_type=f32,
        )
        summed_ref[k * VDIM : (k + 1) * VDIM, :] = summed[NOPE:]


def further_kernel(
    span, count, kv_width, last, query_ref, summed_ref, peak_ref, total_ref, limits, w_kv_ref,
    piece_ref, *refs,
):
    outs, keys = refs[:-1], refs[-1]
    heads = count // span
    column = lax.axis_index("col")
    group = summed_ref.shape[1]
    wide = kv_width + ROPE
    keys[:wide, :] = piece_ref[...]
    keys[wide:, :] = limits[...]
    peak, total, mixed = weigh(query_ref[...], keys[...], None, None, kv_width)
    scale = 1.0 / math.sqrt(NOPE + ROPE)
    top = jnp.maximum(peak, peak_ref[...])
    before = jnp.exp((peak_ref[...] - top) * scale)
    after = jnp.exp((peak - top) * scale)
    total = total_ref[...] * before + total * after
    stats = []
    for k in range(heads):
        lanes = slice(k * group, (k + 1) * group)
        summed = lax.dot_general(
            lifted(w_kv_ref, column, k, span), mixed[:, lanes],
            (((0,), (0,)), ((), ())), preferred_element_type=f32,
        )
        summed = (
            summed_ref[k * VDIM : (k + 1) * VDIM, :] * before[:, lanes]
            + summed[NOPE:] * after[:, lanes]
        )
        outs[0][k * VDIM : (k + 1) * VDIM, :] = summed.astype(outs[0].dtype)
        stats += split3(top[:, lanes]) + split3(total[:, lanes])
        stats += [jnp.zeros_like(total[:, lanes])] * 2
    if last:
        outs[0][heads * VDIM :, :] = jnp.concatenate(stats, axis=0).astype(bf16)
        outs[1][: outs[0].shape[0], :] = outs[0][...]
        outs[1][outs[0].shape[0] :, :] = jnp.zeros_like(outs[1][outs[0].shape[0] :, :])
    else:
        outs[1][...] = top
        outs[2][...] = total


def out_kernel(span, count, width, wide, alive_ref, *refs):
    half = count // 2
    heads = count // span
    columns, refs = refs[:half], refs[half:]
    states, (mine_ref, other_ref, attended, weights) = refs[:half], refs[half:]
    scale = 1.0 / math.sqrt(NOPE + ROPE)
    for i in range(half):
        own = columns[i].shape[0]
        for p in range(VDIM // own):
            lane = padded(wide) + p * padded(2 * width)
            row = i * VDIM + p * own
            weights[row : row + own, :] = columns[i][:, lane : lane + 2 * width].astype(f32)
        parts = []
        for k in range(heads):
            ref = states[i ^ (k * span // 2)]
            lanes = ref[heads * VDIM :, :].astype(f32)[8 * k : 8 * k + 6]
            parts.append(
                (
                    ref[k * VDIM : (k + 1) * VDIM, :].astype(f32),
                    lanes[0:1] + lanes[1:2] + lanes[2:3],
                    lanes[3:4] + lanes[4:5] + lanes[5:6],
                )
            )
        peak = functools.reduce(jnp.maximum, [p[1] for p in parts])
        total = 0.0
        summed = 0.0
        for part in parts:
            factor = jnp.exp((part[1] - peak) * scale)
            total += part[2] * factor
            summed += part[0] * factor
        factor = jnp.where(alive_ref[...] > 0, 1.0 / total, 0.0)
        attended[i * VDIM : (i + 1) * VDIM, :] = (summed * factor).astype(bf16)
    product = lax.dot_general(
        weights[...].astype(bf16), attended[...], (((0,), (0,)), ((), ())), preferred_element_type=f32
    )
    low, high = product[:width], product[width:]
    core = lax.axis_index("col") & 1
    mine_ref[...] = jnp.where(core == 0, low, high)
    other_ref[...] = jnp.where(core == 0, high, low).astype(bf16)


def body(
    tokens, w_down, q_gain, kv_gain, w_q_up, w_kv_up, w_out, latent_cache,
    cache_len, new_len, page_table, home_slot,
):
    count = lax.axis_size("col")
    rows = lax.axis_size("row")
    group = tokens.shape[0]
    own = group // count
    q_width, kv_width, wide = q_gain.shape[0], kv_gain.shape[0], w_down.shape[1]
    span = min(SPAN, count)
    half = count // 2
    heads = count // span
    cols = w_out.shape[1] // count
    piece = latent_cache.shape[1]
    page = piece * count // page_table.shape[1]

    def swap(value, d):
        return lax.ppermute(value, "col", [(s, s ^ d) for s in range(count)])

    def call(kernel, name, shapes, operands, scratch=(), flops=1000, scalars=0):
        single = not isinstance(shapes, list)
        result = pl.pallas_call(
            kernel,
            out_shape=shapes,
            in_specs=[SMEM] * scalars + [VMEM] * (len(operands) - scalars),
            out_specs=VMEM if single else [VMEM] * len(shapes),
            scratch_shapes=list(scratch),
            compiler_params=PARAMS,
            cost_estimate=cost(flops, 1000),
            name=name,
        )(*operands)
        return result if single else list(result)

    shape = jax.ShapeDtypeStruct
    held = latent_cache[0].T

    def pass_on(value, d):
        return lax.ppermute(value, "row", [(s, (s + d) % rows) for s in range(rows)])

    moved = {0: held}
    for d in range(1, rows // 2 + 1):
        moved[d] = pass_on(moved[d - 1], 1)
        if rows - d > d:
            moved[rows - d] = pass_on(moved[(rows - d + 1) % rows], -1)
    query_weights = [w_q_up.T] + [swap(w_q_up.T, d) for d in range(span, count, span)]
    even, odd = call(
        functools.partial(down_kernel, count, own), "down",
        [shape((half, own, wide), bf16)] * 2, (tokens.T, w_down),
        [pltpu.VMEM((group, wide), f32)],
    )
    length = padded(wide) + VDIM // own * padded(2 * cols)
    paired = call(
        functools.partial(sum_kernel, count, wide), "sum",
        [shape((own, length), bf16)] * half, (even, swap(odd, 1), w_out),
    )
    paired[0], home_slot = lax.optimization_barrier((paired[0], home_slot))
    partial = [paired[0]] + [swap(paired[k], 2 * k) for k in range(1, half)]
    own_cos, own_sin, cosine, sine, limits, fresh_limits, alive, choice, q_scale, kv_scale = call(
        functools.partial(prepare_kernel, span, count, own, page), "prepare",
        [shape((own, ROPE // 2), f32)] * 2
        + [shape((ROPE // 2, group), f32)] * 2
        + [shape((EXTRA, span * piece), bf16), shape((span * own, group), f32)]
        + [shape((1, group), f32), shape((rows, group), f32)]
        + [shape((1, q_width), f32), shape((1, kv_width), f32)],
        (home_slot, cache_len, new_len, page_table, q_gain[None], kv_gain[None]),
        [pltpu.SMEM((page_table.shape[1],), jnp.int32)], scalars=4,
    )
    block = call(
        functools.partial(norm_kernel, q_width, kv_width), "norm", shape((own, padded(wide) + 128), bf16),
        (own_cos, own_sin, q_scale, kv_scale, *partial),
    )
    blocks = [None] * count
    for d in range(0, count, 2):
        blocks[d] = swap(block, d) if d else block
    last = rows // 2
    block, moved[last], moved[rows - 1] = lax.optimization_barrier((block, moved[last], moved[rows - 1]))
    blocks[0] = block
    cache = held
    for d in range(1, rows):
        cache = jnp.where(choice[d, :piece] > 0, moved[d], cache)
    for d in range(0, count, 2):
        blocks[d + 1] = swap(blocks[d], 1)
    pieces = [cache, swap(cache, 1)]
    held_as = f32 if own % 16 else bf16
    deep = kv_width + ROPE + EXTRA
    lines = shape((1, heads * group), f32)
    partial_state = [shape((heads * VDIM, group), f32), lines, lines]
    query, *state = call(
        functools.partial(begin_kernel, span, count, own, q_width, kv_width), "begin",
        [shape((deep, heads * group), bf16)] + partial_state,
        (cosine, sine, limits, fresh_limits, w_kv_up, *query_weights, *blocks, *pieces[:2]),
        [
            pltpu.VMEM((group, q_width), held_as),
            pltpu.VMEM((span * own, kv_width + ROPE), held_as),
            pltpu.VMEM((deep, 2 * piece), bf16),
        ],
        1000,
    )
    for d in range(2, span, 2):
        beyond = swap(cache, d)
        beyond, query = lax.optimization_barrier((beyond, query))
        for turn, keys in enumerate((beyond, swap(beyond, 1))):
            last = d + turn == span - 1
            state = call(
                functools.partial(further_kernel, span, count, kv_width, last), "further",
                [shape((heads * (VDIM + 8) + rows_more, group), bf16) for rows_more in (0, 16)]
                if last
                else partial_state,
                (
                    query, *state, limits[:, (d + turn) * piece : (d + turn + 1) * piece],
                    w_kv_up, keys,
                ),
                [pltpu.VMEM((deep, piece), bf16)],
                1_000_000_000,
            )
    state, far = state
    states = [state] + [swap(far if d & (d - 1) else state, d) for d in range(2, count, 2)]
    mine, other = call(
        functools.partial(out_kernel, span, count, cols, wide), "out",
        [shape((cols, group), f32), shape((cols, group), bf16)],
        (alive, *partial, *states),
        [
            pltpu.VMEM((half * VDIM, group), bf16),
            pltpu.VMEM((half * VDIM, 2 * cols), f32),
        ],
    )
    return (mine + swap(other, 1).astype(f32)).astype(bf16).T


def solution(mesh):
    return jax.shard_map(
        body,
        mesh=mesh,
        in_specs=(
            P("row", "col"),
            P("col", None),
            P(),
            P(),
            P(None, "col"),
            P(),
            P("col", None),
            P("row", "col", None),
            P(),
            P(),
            P(),
            P(),
        ),
        out_specs=P("row", "col"),
        check_vma=False,
    )
```

```python
import functools
import math

import jax
import jax.numpy as jnp
from jax import lax
from jax.experimental import pallas as pl
from jax.experimental.pallas import tpu as pltpu
from jax.sharding import PartitionSpec as P

NOPE = 64
ROPE = 32
VDIM = 64
HEAD = NOPE + VDIM
SPAN = 4
EXTRA = 16
epsilon = 1e-05
SCALE = math.log2(math.e) / math.sqrt(NOPE + ROPE)
MASKED = -1e30
FLOOR = -1e29

bf16 = jnp.bfloat16
f32 = jnp.float32
VMEM = pl.BlockSpec(memory_space=pltpu.VMEM)
SMEM = pl.BlockSpec(memory_space=pltpu.SMEM)
PARAMS = pltpu.CompilerParams(vmem_limit_bytes=32 * 1024 * 1024)


def cost(flops, moved, special=0):
    return pl.CostEstimate(flops=flops, bytes_accessed=moved, transcendentals=special)


def near_offsets(span, count):
    high = count // (span // 2)
    return [i // 2 * high + i % 2 for i in range(span)]


def across_offsets(span, count):
    return [2 * k for k in range(count // span)]


def padded(lanes):
    return -(-lanes // 128) * 128


def rotate(values, cosine, sine, axis):
    half = ROPE // 2
    first = lax.slice_in_dim(values, 0, half, axis=axis)
    second = lax.slice_in_dim(values, half, 2 * half, axis=axis)
    return jnp.concatenate(
        [first * cosine - second * sine, second * cosine + first * sine], axis=axis
    )


def down_kernel(count, own, tokens_ref, w_ref, even_ref, odd_ref, sums):
    column = lax.axis_index("col")
    sums[...] = lax.dot_general(
        tokens_ref[...], w_ref[...], (((0,), (0,)), ((), ())), preferred_element_type=f32
    )
    for j in range(count):
        start = pl.multiple_of((column ^ j) * own, own)
        target = odd_ref if j % 2 else even_ref
        target[j // 2] = sums[pl.ds(start, own), :].astype(bf16)


def prepare_kernel(
    span, count, own, page, home_ref, cached_ref, live_ref, page_ref, q_gain_ref, kv_gain_ref,
    own_cos, own_sin, cosine, sine, limits, fresh_limits, alive, choice, q_gain, kv_gain, logical,
):
    q_gain[...] = q_gain_ref[...]
    kv_gain[...] = kv_gain_ref[...]
    column = lax.axis_index("col")
    near = near_offsets(span, count)
    row = lax.axis_index("row")
    slot = home_ref[row]
    live = live_ref[row]
    cached = cached_ref[slot]
    rows = choice.shape[0]
    group = count * own
    half = ROPE // 2
    rate = -2.0 * math.log(10000.0) / ROPE

    place = cached + column * own + lax.broadcasted_iota(jnp.int32, (own, half), 0)
    step = lax.broadcasted_iota(jnp.int32, (own, half), 1).astype(f32)
    angle = place.astype(f32) * jnp.exp(step * rate)
    own_cos[...] = jnp.cos(angle)
    own_sin[...] = jnp.sin(angle)
    place = cached + lax.broadcasted_iota(jnp.int32, (half, group), 1)
    step = lax.broadcasted_iota(jnp.int32, (half, group), 0).astype(f32)
    angle = place.astype(f32) * jnp.exp(step * rate)
    cosine[...] = jnp.cos(angle)
    sine[...] = jnp.sin(angle)

    for l in range(page_ref.shape[1]):
        logical[page_ref[slot, l]] = l
    per_piece = limits.shape[1] // span // page
    offset = lax.broadcasted_iota(jnp.int32, (EXTRA, page), 1)
    line = lax.broadcasted_iota(jnp.int32, (EXTRA, page), 0)
    for j in range(span):
        for p in range(per_piece):
            seen = offset < cached - logical[(column ^ near[j]) * per_piece + p] * page
            start = (j * per_piece + p) * page
            limits[:, start : start + page] = jnp.where(seen | (line > 0), 0.0, MASKED).astype(bf16)
    query_id = lax.broadcasted_iota(jnp.int32, (own, group), 1)
    offset = lax.broadcasted_iota(jnp.int32, (own, group), 0)
    for j in range(span):
        fresh_id = (column ^ near[j]) * own + offset
        seen = (fresh_id <= query_id) & (fresh_id < live)
        fresh_limits[j * own : (j + 1) * own, :] = jnp.where(seen, 0.0, MASKED)
    token = lax.broadcasted_iota(jnp.int32, (1, group), 1)
    alive[...] = jnp.where(token < live, 1.0, 0.0)
    source = lax.broadcasted_iota(jnp.int32, choice.shape, 0)
    source = jnp.where(row >= source, row - source, row - source + rows)
    choice[...] = jnp.where(source == slot, 1.0, 0.0)


def sum_kernel(count, wide, even_ref, odd_ref, w_out_ref, *outs):
    half = count // 2
    own = even_ref.shape[1]
    width = 2 * (w_out_ref.shape[1] // count)
    chip = lax.axis_index("col") // 2
    for i, ref in enumerate(outs):
        ref[:, :wide] = (even_ref[i].astype(f32) + odd_ref[i].astype(f32)).astype(bf16)
        start = (chip ^ i) * width
        if width % 128 == 0:
            taken = w_out_ref[:, pl.ds(pl.multiple_of(start, 128), width)]
        else:
            taken = w_out_ref[:, :width]
            for k in range(1, half):
                taken = jnp.where(chip ^ i == k, w_out_ref[:, k * width : (k + 1) * width], taken)
        for p in range(taken.shape[0] // own):
            lane = padded(wide) + p * padded(width)
            ref[:, lane : lane + width] = taken[p * own : (p + 1) * own]


def norm_kernel(q_width, kv_width, cos_ref, sin_ref, q_gain_ref, kv_gain_ref, *refs):
    out_ref = refs[-1]
    wide = q_width + kv_width + ROPE
    total = refs[0][:, :wide].astype(f32)
    for ref in refs[1:-1]:
        total += ref[:, :wide].astype(f32)

    def scaled(values, gain):
        mean = jnp.mean(values * values, axis=-1, keepdims=True)
        return values * lax.rsqrt(mean + epsilon) * gain

    out_ref[:, :q_width] = scaled(total[:, :q_width], q_gain_ref[...]).astype(bf16)
    out_ref[:, q_width : q_width + kv_width] = scaled(
        total[:, q_width : q_width + kv_width], kv_gain_ref[...]
    ).astype(bf16)
    out_ref[:, q_width + kv_width : wide] = rotate(
        total[:, q_width + kv_width :], cos_ref[...], sin_ref[...], 1
    ).astype(bf16)
    out_ref[:, wide:] = jnp.zeros_like(out_ref[:, wide:])


def split3(value):
    high = value.astype(bf16).astype(f32)
    middle = (value - high).astype(bf16).astype(f32)
    return [high, middle, value - high - middle]


def weigh(query, keys, fresh, fresh_bias, kv_width):
    scores = [
        lax.dot_general(keys, query, (((0,), (0,)), ((), ())), preferred_element_type=f32)
    ]
    if fresh is not None:
        new = jnp.dot(fresh, query[: fresh.shape[1]], preferred_element_type=f32)
        scores.append(new + jnp.concatenate([fresh_bias] * (new.shape[1] // fresh_bias.shape[1]), 1))
    peak = functools.reduce(jnp.maximum, [jnp.max(s, 0, keepdims=True) for s in scores])
    peak = jnp.maximum(peak, FLOOR)
    weights = [jnp.exp2(s - peak) for s in scores]
    total = sum(jnp.sum(w, 0, keepdims=True) for w in weights)
    mixed = jnp.dot(keys[:kv_width], weights[0].astype(bf16), preferred_element_type=f32)
    if fresh is not None:
        mixed += lax.dot_general(
            fresh[:, :kv_width], weights[1].astype(bf16),
            (((0,), (0,)), ((), ())), preferred_element_type=f32,
        )
    return peak, total, mixed


def lifted(w_kv_ref, column, k, count, span):
    head = column ^ across_offsets(span, count)[k]
    return w_kv_ref[:, pl.ds(pl.multiple_of(head * HEAD, HEAD), HEAD)]


def begin_kernel(
    span, count, own, q_width, kv_width, cos_ref, sin_ref, limits, fresh_limits, w_kv_ref, *refs
):
    heads = count // span
    weights, refs = refs[:heads], refs[heads:]
    blocks, refs = refs[:count], refs[count:]
    pieces, (query_ref, mixed_ref, peak_ref, total_ref, query_rows, fresh, keys) = refs[:2], refs[2:]
    column = lax.axis_index("col")
    group = count * own
    piece = pieces[0].shape[1]
    wide = kv_width + ROPE
    for j in range(count):
        start = pl.multiple_of((column ^ j) * own, own)
        query_rows[pl.ds(start, own), :] = blocks[j][:, :q_width].astype(query_rows.dtype)
    for j, offset in enumerate(near_offsets(span, count)):
        latents = blocks[offset][:, q_width : q_width + wide]
        fresh[j * own : (j + 1) * own, :] = latents.astype(fresh.dtype)
    for j in range(2):
        keys[:wide, j * piece : (j + 1) * piece] = pieces[j][...]
    keys[wide:, :] = limits[:, : 2 * piece]
    latent = query_rows[...].astype(bf16)
    line = lax.broadcasted_iota(jnp.int32, (EXTRA, group), 0)
    first_row = jnp.where(line == 0, 1.0, 0.0).astype(bf16)
    for k in range(heads):
        projected = lax.dot_general(
            weights[k][...], latent, (((1,), (1,)), ((), ())), preferred_element_type=f32
        )
        turned = rotate(projected[NOPE:], cos_ref[...], sin_ref[...], 0)
        plain = jnp.dot(
            lifted(w_kv_ref, column, k, count, span)[:, :NOPE],
            projected[:NOPE].astype(bf16), preferred_element_type=f32,
        )
        lanes = slice(k * group, (k + 1) * group)
        query_ref[:kv_width, lanes] = (plain * SCALE).astype(bf16)
        query_ref[kv_width:wide, lanes] = (turned * SCALE).astype(bf16)
        query_ref[wide:, lanes] = first_row
    peak, total, mixed = weigh(
        query_ref[...], keys[...], fresh[...].astype(bf16), fresh_limits[...], kv_width
    )
    peak_ref[...] = peak
    total_ref[...] = total
    mixed_ref[...] = mixed


def further_kernel(
    span, count, kv_width, last, query_ref, mixed_ref, peak_ref, total_ref, limits, w_kv_ref,
    piece_ref, *refs,
):
    outs, keys = refs[:-1], refs[-1]
    heads = count // span
    column = lax.axis_index("col")
    group = mixed_ref.shape[1] // heads
    wide = kv_width + ROPE
    keys[:wide, :] = piece_ref[...]
    keys[wide:, :] = limits[...]
    peak, total, mixed = weigh(query_ref[...], keys[...], None, None, kv_width)
    top = jnp.maximum(peak, peak_ref[...])
    before = jnp.exp2(peak_ref[...] - top)
    after = jnp.exp2(peak - top)
    total = total_ref[...] * before + total * after
    mixed = mixed_ref[...] * before + mixed * after
    if not last:
        outs[0][...] = mixed
        outs[1][...] = top
        outs[2][...] = total
        return
    mixed = mixed.astype(bf16)
    stats = []
    for k in range(heads):
        lanes = slice(k * group, (k + 1) * group)
        summed = lax.dot_general(
            lifted(w_kv_ref, column, k, count, span), mixed[:, lanes],
            (((0,), (0,)), ((), ())), preferred_element_type=f32,
        )
        outs[0][k * VDIM : (k + 1) * VDIM, :] = summed[NOPE:].astype(bf16)
        stats += split3(top[:, lanes]) + split3(total[:, lanes])
        stats += [jnp.zeros_like(total[:, lanes])] * 2
    outs[0][heads * VDIM :, :] = jnp.concatenate(stats, axis=0).astype(bf16)
    outs[1][: outs[0].shape[0], :] = outs[0][...]
    outs[1][outs[0].shape[0] :, :] = jnp.zeros_like(outs[1][outs[0].shape[0] :, :])


def out_kernel(span, count, width, wide, alive_ref, *refs):
    half = count // 2
    heads = count // span
    columns, refs = refs[:half], refs[half:]
    states, (mine_ref, other_ref, attended, weights) = refs[:half], refs[half:]
    for i in range(half):
        own = columns[i].shape[0]
        for p in range(VDIM // own):
            lane = padded(wide) + p * padded(2 * width)
            row = i * VDIM + p * own
            weights[row : row + own, :] = columns[i][:, lane : lane + 2 * width].astype(
                weights.dtype
            )
        parts = []
        for k in range(heads):
            ref = states[i ^ (across_offsets(span, count)[k] // 2)]
            lanes = ref[heads * VDIM :, :].astype(f32)[8 * k : 8 * k + 6]
            parts.append(
                (
                    ref[k * VDIM : (k + 1) * VDIM, :].astype(f32),
                    lanes[0:1] + lanes[1:2] + lanes[2:3],
                    lanes[3:4] + lanes[4:5] + lanes[5:6],
                )
            )
        peak = functools.reduce(jnp.maximum, [p[1] for p in parts])
        total = 0.0
        summed = 0.0
        for part in parts:
            factor = jnp.exp2(part[1] - peak)
            total += part[2] * factor
            summed += part[0] * factor
        factor = jnp.where(alive_ref[...] > 0, 1.0 / total, 0.0)
        attended[i * VDIM : (i + 1) * VDIM, :] = (summed * factor).astype(bf16)
    product = lax.dot_general(
        weights[...].astype(bf16), attended[...], (((0,), (0,)), ((), ())), preferred_element_type=f32
    )
    low, high = product[:width], product[width:]
    core = lax.axis_index("col") & 1
    mine_ref[...] = jnp.where(core == 0, low, high)
    other_ref[...] = jnp.where(core == 0, high, low).astype(bf16)


def body(
    tokens, w_down, q_gain, kv_gain, w_q_up, w_kv_up, w_out, latent_cache,
    cache_len, new_len, page_table, home_slot,
):
    count = lax.axis_size("col")
    rows = lax.axis_size("row")
    group = tokens.shape[0]
    own = group // count
    q_width, kv_width, wide = q_gain.shape[0], kv_gain.shape[0], w_down.shape[1]
    span = min(SPAN, count)
    half = count // 2
    heads = count // span
    cols = w_out.shape[1] // count
    piece = latent_cache.shape[1]
    page = piece * count // page_table.shape[1]

    def swap(value, d):
        return lax.ppermute(value, "col", [(s, s ^ d) for s in range(count)])

    def call(kernel, name, shapes, operands, scratch=(), flops=1000, scalars=0):
        single = not isinstance(shapes, list)
        result = pl.pallas_call(
            kernel,
            out_shape=shapes,
            in_specs=[SMEM] * scalars + [VMEM] * (len(operands) - scalars),
            out_specs=VMEM if single else [VMEM] * len(shapes),
            scratch_shapes=list(scratch),
            compiler_params=PARAMS,
            cost_estimate=cost(flops, 1000),
            name=name,
        )(*operands)
        return result if single else list(result)

    shape = jax.ShapeDtypeStruct
    held = latent_cache[0].T

    def pass_on(value, d):
        return lax.ppermute(value, "row", [(s, (s + d) % rows) for s in range(rows)])

    moved = {0: held}
    for d in range(1, rows // 2 + 1):
        moved[d] = pass_on(moved[d - 1], 1)
        if rows - d > d:
            moved[rows - d] = pass_on(moved[(rows - d + 1) % rows], -1)
    query_weights = [w_q_up.T] + [swap(w_q_up.T, d) for d in across_offsets(span, count)[1:]]
    even, odd = call(
        functools.partial(down_kernel, count, own), "down",
        [shape((half, own, wide), bf16)] * 2, (tokens.T, w_down),
        [pltpu.VMEM((group, wide), f32)],
    )
    length = padded(wide) + VDIM // own * padded(2 * cols)
    paired = call(
        functools.partial(sum_kernel, count, wide), "sum",
        [shape((own, length), bf16)] * half, (even, swap(odd, 1), w_out),
    )
    paired[0], home_slot = lax.optimization_barrier((paired[0], home_slot))
    partial = [paired[0]] + [swap(paired[k], 2 * k) for k in range(1, half)]
    own_cos, own_sin, cosine, sine, limits, fresh_limits, alive, choice, q_scale, kv_scale = call(
        functools.partial(prepare_kernel, span, count, own, page), "prepare",
        [shape((own, ROPE // 2), f32)] * 2
        + [shape((ROPE // 2, group), f32)] * 2
        + [shape((EXTRA, span * piece), bf16), shape((span * own, group), f32)]
        + [shape((1, group), f32), shape((rows, piece), f32)]
        + [shape((1, q_width), f32), shape((1, kv_width), f32)],
        (home_slot, cache_len, new_len, page_table, q_gain[None], kv_gain[None]),
        [pltpu.SMEM((page_table.shape[1],), jnp.int32)], scalars=4,
    )
    block = call(
        functools.partial(norm_kernel, q_width, kv_width), "norm", shape((own, padded(wide) + 128), bf16),
        (own_cos, own_sin, q_scale, kv_scale, *partial),
    )
    blocks = [None] * count
    for d in range(0, count, 2):
        blocks[d] = swap(block, d) if d else block
    last = rows // 2
    block, moved[last], moved[rows - 1] = lax.optimization_barrier((block, moved[last], moved[rows - 1]))
    blocks[0] = block
    cache = held
    for d in range(1, rows):
        cache = jnp.where(choice[d] > 0, moved[d], cache)
    for d in range(0, count, 2):
        blocks[d + 1] = swap(blocks[d], 1)
    pieces = [cache, swap(cache, 1)]
    held_as = f32 if own % 16 else bf16
    deep = kv_width + ROPE + EXTRA
    lines = shape((1, heads * group), f32)
    partial_state = [shape((kv_width, heads * group), f32), lines, lines]
    query, *state = call(
        functools.partial(begin_kernel, span, count, own, q_width, kv_width), "begin",
        [shape((deep, heads * group), bf16)] + partial_state,
        (cosine, sine, limits, fresh_limits, w_kv_up, *query_weights, *blocks, *pieces[:2]),
        [
            pltpu.VMEM((group, q_width), held_as),
            pltpu.VMEM((span * own, kv_width + ROPE), held_as),
            pltpu.VMEM((deep, 2 * piece), bf16),
        ],
        1000,
    )
    near = near_offsets(span, count)
    for d in range(2, span, 2):
        beyond = swap(cache, near[d])
        beyond, query = lax.optimization_barrier((beyond, query))
        for turn, keys in enumerate((beyond, swap(beyond, 1))):
            last = d + turn == span - 1
            state = call(
                functools.partial(further_kernel, span, count, kv_width, last), "further",
                [shape((heads * (VDIM + 8) + rows_more, group), bf16) for rows_more in (0, 16)]
                if last
                else partial_state,
                (
                    query, *state, limits[:, (d + turn) * piece : (d + turn + 1) * piece],
                    w_kv_up, keys,
                ),
                [pltpu.VMEM((deep, piece), bf16)],
                1_000_000_000,
            )
    state, far = state
    states = [state] + [swap(far if d & (d - 1) else state, d) for d in range(2, count, 2)]
    mine, other = call(
        functools.partial(out_kernel, span, count, cols, wide), "out",
        [shape((cols, group), f32), shape((cols, group), bf16)],
        (alive, *partial, *states),
        [
            pltpu.VMEM((half * VDIM, group), bf16),
            pltpu.VMEM((half * VDIM, 2 * cols), held_as),
        ],
    )
    return (mine + swap(other, 1).astype(f32)).astype(bf16).T


def solution(mesh):
    return jax.shard_map(
        body,
        mesh=mesh,
        in_specs=(
            P("row", "col"),
            P("col", None),
            P(),
            P(),
            P(None, "col"),
            P(),
            P("col", None),
            P("row", "col", None),
            P(),
            P(),
            P(),
            P(),
        ),
        out_specs=P("row", "col"),
        check_vma=False,
    )
```
